128 devices in a mesh: ctx: 32 (over x, y_hi, z), tp: 4 (over y_lo, core).
Axes of the slice: x: 4, y: 4 (y_hi: 2, y_lo: 2; y = y_hi * 2 + y_lo), z: 4, core: 2. Of those that a mesh axis runs over, the one named last changes fastest.
Arguments:
- queries: bfloat16 [512, 16384], P('ctx', 'tp'), may hold values from -27 to 27
- new_keys: bfloat16 [512, 1024], P('ctx', 'tp'), may hold values from -5 to 5
- new_values: bfloat16 [512, 1024], P('ctx', 'tp'), may hold values from -5 to 5
- cache_keys: bfloat16 [65536, 1024], P('ctx', 'tp'), may hold values from -10 to 10
- cache_values: bfloat16 [65536, 1024], P('ctx', 'tp'), may hold values from -5 to 5
- cache_lens: int32 [32], P('ctx'), may hold values from 1 to 2048, 33792 in all
- out_weight: bfloat16 [16384, 16384], P('tp', 'ctx'), may hold values from -0.046875 to 0.046875
Outputs:
- attention_update: bfloat16 [512, 16384], P('tp', 'ctx')
The draws below stay inside these ranges and needn't reach their ends.
Inputs may be any that keep to these rules, and one draw needn't show every extreme that they name: `cache_lens`: the largest entry equals 2048; the entries sum to 33792.
All inputs are finite; a program needn't handle non-finite values. No bound on the sum of `cache_lens` on one device may be relied on, other than what follows from the above.
Results may differ from the reference program's by a relative error of at most 0.02.
Values may be sent and summed in bfloat16 or wider, within the bound.
A program may use at most 576 MiB of HBM per device.

```python
import math
import jax
import jax.numpy as jnp
import numpy as np
from jax import lax

D = 16384
HEADS = 128
KVH = 8
HD = 128
Q_DEV = 16
CACHE_DEV = 2048
NEW = 512
CACHE_TOTAL = 65536
N_CTX = 32


def draw_queries(key, part):
    key = jax.random.fold_in(key, 5)
    values = jnp.clip(jax.random.normal(key, (NEW, HEADS * HD), jnp.float32), -5.0, 5.0)
    return values.astype(jnp.bfloat16)


def draw_cache_keys(key, part):
    key = jax.random.fold_in(key, 9)
    main_key = jax.random.fold_in(key, 1)
    values = jnp.clip(jax.random.normal(main_key, (CACHE_TOTAL, KVH * HD), jnp.float32), -5.0, 5.0)
    return values.astype(jnp.bfloat16)


def levels(stream_key, extent, pieces, low, high):
    loudness = 1.0
    for dim, parts in pieces:
        heights = jax.random.uniform(jax.random.fold_in(jax.random.fold_in(stream_key, 6), dim), (parts,), jnp.float32, low / len(pieces), high / len(pieces))
        loudness = loudness * jnp.repeat(jnp.exp(heights), extent[dim] // parts).reshape((-1,) + (1,) * (len(extent) - 1 - dim))
    return loudness


def split_up(number_of, total, limit, skew):
    loads = [(1 << 20) // math.isqrt(standing ** skew) + 1 for standing in range(2, number_of + 1)]
    spare, holding = total - limit - (number_of - 1), [1] * (number_of - 1)
    while spare > 0:
        movable = [i for i in range(number_of - 1) if holding[i] < limit]
        whole, budget = sum([loads[i] for i in movable]), spare
        for i in movable:
            more = min(limit - holding[i], max(1, budget * loads[i] // whole), spare)
            holding[i] = holding[i] + more
            spare = spare - more
    return np.array([limit] + holding)


def ragged_sizes(rng, number_of, total, limit, lean):
    if number_of == 2:
        one = jax.random.randint(rng, (), max(1, total - limit), min(limit, total - 1) + 1)
        return jnp.stack([one, total - one])
    tallies = jnp.asarray(split_up(number_of, total, limit, lean), jnp.int32)
    twos = (number_of - 1) // 2
    donor, receiver = tallies[1:1 + 2 * twos:2], tallies[2:2 + 2 * twos:2]
    room = jnp.minimum(donor - 1, limit - receiver)
    passed = jax.random.randint(jax.random.fold_in(rng, 1), (twos,), 0, 1 << 20) % (room + 1)
    tallies = tallies.at[1:1 + 2 * twos:2].set(donor - passed).at[2:2 + 2 * twos:2].set(receiver + passed)
    return tallies[jax.random.permutation(jax.random.fold_in(rng, 2), number_of)]


def gaussian(stream_key, shape, deviation, limit, pieces=(), held_as=jnp.bfloat16):
    loudness = levels(stream_key, shape, pieces, -0.22, 0.18) if pieces else 1.0
    values = jax.random.normal(stream_key, shape, jnp.float32) * deviation * loudness
    return jnp.minimum(jnp.maximum(values, -limit), limit).astype(held_as)


def setup_inputs(seed: int = 0) -> dict:
    splits = jax.random.split(jax.random.key(seed), 8)
    queries = draw_queries(jax.random.fold_in(splits[7], 71), 0)
    new_keys = gaussian(splits[1], (NEW, KVH * HD), 1.0, 5.0, ((0, 32), (1, 4)))
    new_values = gaussian(splits[2], (NEW, KVH * HD), 1.0, 5.0, ((0, 32), (1, 4)))
    cache_keys = draw_cache_keys(jax.random.fold_in(splits[7], 71), 0)
    cache_values = gaussian(splits[4], (CACHE_TOTAL, KVH * HD), 1.0, 5.0, ((0, 32), (1, 4)))
    cache_lens = ragged_sizes(splits[5], N_CTX, (N_CTX + 1) * CACHE_DEV // 2, CACHE_DEV, 2).astype(jnp.int32)
    out_weight = gaussian(splits[6], (HEADS * HD, D), (HEADS * HD) ** -0.5, 0.046875, ((0, 4), (1, 32)))
    return {"queries": queries, "new_keys": new_keys, "new_values": new_values, "cache_keys": cache_keys, "cache_values": cache_values, "cache_lens": cache_lens, "out_weight": out_weight}


NEG = -1e+30

def rounded(values):
    return lax.optimization_barrier(values.astype(jnp.bfloat16)).astype(jnp.float32)

def reference(queries, new_keys, new_values, cache_keys, cache_values, cache_lens, out_weight):
    group = HEADS // KVH
    blocks_count = NEW // Q_DEV
    scale = 1.0 / math.sqrt(HD)
    slot_index = jnp.arange(CACHE_TOTAL, dtype=jnp.int32)
    live = slot_index % CACHE_DEV < cache_lens[slot_index // CACHE_DEV]
    live_mask = live.reshape(blocks_count, CACHE_DEV)[None, None, None, :, :]
    keys_old = cache_keys.astype(jnp.float32).reshape(blocks_count, CACHE_DEV, KVH, HD)
    values_old = cache_values.astype(jnp.float32).reshape(blocks_count, CACHE_DEV, KVH, HD)
    keys_new = new_keys.astype(jnp.float32).reshape(blocks_count, Q_DEV, KVH, HD)
    values_new = new_values.astype(jnp.float32).reshape(blocks_count, Q_DEV, KVH, HD)
    blocks = queries.astype(jnp.float32).reshape(blocks_count, Q_DEV, KVH, group, HD)
    starts = jnp.arange(blocks_count, dtype=jnp.int32) * Q_DEV
    key_place = jnp.arange(NEW, dtype=jnp.int32).reshape(blocks_count, Q_DEV)

    def one_block(pair):
        query, start = pair
        places = start + jnp.arange(Q_DEV, dtype=jnp.int32)
        new_mask = (key_place[None, :, :] <= places[:, None, None])[:, None, None, :, :]
        old_scores = jnp.einsum('qgrd,ckgd->qgrck', query, keys_old) * scale
        new_scores = jnp.einsum('qgrd,ckgd->qgrck', query, keys_new) * scale
        peak = jnp.maximum(lax.optimization_barrier(jnp.max(jnp.where(live_mask, old_scores, NEG), axis=-1)), lax.optimization_barrier(jnp.max(jnp.where(new_mask, new_scores, NEG), axis=-1)))
        probs_old = jnp.where(live_mask, jnp.exp(old_scores - peak[..., None]), 0.0)
        probs_new = jnp.where(new_mask, jnp.exp(new_scores - peak[..., None]), 0.0)
        total = lax.optimization_barrier(jnp.sum(probs_old, axis=-1)) + lax.optimization_barrier(jnp.sum(probs_new, axis=-1))
        summed = jnp.einsum('qgrck,ckgd->qgrcd', rounded(probs_old), values_old)
        summed = summed + jnp.einsum('qgrck,ckgd->qgrcd', rounded(probs_new), values_new)
        partial_value = rounded(summed / total[..., None])
        log_total = peak + jnp.log(total)
        top = lax.optimization_barrier(jnp.max(log_total, axis=-1))
        weights = jnp.exp(log_total - top[..., None])
        joined = lax.optimization_barrier(jnp.sum(partial_value * weights[..., None], axis=-2)) / lax.optimization_barrier(jnp.sum(weights, axis=-1))[..., None]
        return joined.reshape(Q_DEV, HEADS * HD).astype(jnp.bfloat16)
    heads_out = lax.map(one_block, (blocks, starts)).reshape(NEW, HEADS * HD)
    return jnp.dot(heads_out, out_weight, preferred_element_type=jnp.float32).astype(jnp.bfloat16)
```

```python
import math

import jax
import jax.numpy as jnp
from jax import lax
from jax.experimental import pallas as pl
from jax.experimental.pallas import tpu as pltpu
from jax.sharding import PartitionSpec as P

HD = 128
NX = 4
NZ = 4
ROWS = 16
SLOTS = 2048
HEADS = 8
TOK = NX * NZ * 2 * ROWS
PIECES = 4
PIECE = HEADS // PIECES * HD
SUB = 512
NEG = -1e30
LOG2E = 1.4426950408889634
SCALE = LOG2E / math.sqrt(HD)
F32 = jnp.float32
BF16 = jnp.bfloat16
MESH = pl.DeviceIdType.MESH


def kernel(
    q_hbm, nk_hbm, nv_hbm, ck_hbm, cv_hbm, len_ref, w_hbm, out_ref,
    q, kd, vd, nkd, nvd, lens, bias, s0, s1, sn0, sn1, m0, m1, o1, mx1,
    part, lts, r1o, r1l, s2o, s2l, r2o, r2l, tmp, g, w,
    acc, es1, er1, es2, er2,
    loc, ex_s, ex_r, qa_s, qa_r, rs_s, rs_r, rl_s, rl_r, ag_s, ag_r, e_s, e_r,
):
    ctx = lax.axis_index("ctx")
    tp = lax.axis_index("tp")
    z = lax.rem(ctx, NZ)
    yh = lax.rem(ctx // NZ, 2)
    x = ctx // (2 * NZ)
    core = lax.rem(tp, 2)
    yl = tp // 2
    oh = 1 - yh

    def at(xx, hh, zz, ll, cc):
        return ((xx * 2 + hh) * NZ + zz, ll * 2 + cc)

    partner = at(x, oh, z, yl, core)
    sibling = at(x, yh, z, yl, 1 - core)
    place = ((x, z), (z, x))

    def p_peer(h, d):
        to = lax.rem(place[h][0] + d, 4)
        return to, (at(to, yh, z, yl, core) if h == 0 else at(x, yh, to, yl, core))

    def s_peer(h, d):
        to = lax.rem(place[h][1] + d, 4)
        return to, (at(x, yh, to, yl, core) if h == 0 else at(to, yh, z, yl, core))

    ends = [at(x, yh, z, 1 - yl, core), partner, at(x, oh, z, 1 - yl, core)]

    def local(src, dst, sem):
        return pltpu.make_async_copy(src, dst, sem)

    def remote(src, dst, ssem, rsem, to):
        return pltpu.make_async_remote_copy(
            src_ref=src, dst_ref=dst, send_sem=ssem, recv_sem=rsem, device_id=to, device_id_type=MESH
        )

    def await_bytes(ref, sem):
        pltpu.make_async_copy(ref, ref, sem).wait()

    def cut(start, size):
        return pl.ds(pl.multiple_of(start, size), size)

    mine = [
        local(ck_hbm.at[:, cut(yh * HD, HD)], kd.at[0, :, pl.ds(0, HD)], loc.at[0]),
        local(cv_hbm.at[:, cut(yh * HD, HD)], vd.at[0, :, pl.ds(0, HD)], loc.at[1]),
        local(nk_hbm.at[:, cut(yh * HD, HD)], nkd.at[cut(yh * ROWS, ROWS), pl.ds(0, HD)], loc.at[2]),
        local(nv_hbm.at[:, cut(yh * HD, HD)], nvd.at[cut(yh * ROWS, ROWS), pl.ds(0, HD)], loc.at[3]),
    ]
    for h in range(2):
        mine.append(
            local(
                q_hbm.at[:, cut(yh * 2048 + h * 1024, 1024)],
                q.at[h, place[h][0], place[h][1], cut(yh * ROWS, ROWS)],
                loc.at[4 + h],
            )
        )
    own_w = local(w_hbm.at[cut(yh * 2048, 2048)], w.at[yh], loc.at[6])
    for copy in mine:
        copy.start()
    own_w.start()

    lens[0] = jnp.broadcast_to(len_ref[0], (8, HD))
    nkd[32:HD, :] = jnp.zeros((HD - 32, 2 * HD), BF16)
    nvd[32:HD, :] = jnp.zeros((HD - 32, 2 * HD), BF16)

    barrier = pltpu.get_barrier_semaphore()
    greet = [partner, sibling, ends[0], ends[2]]
    for d in range(1, 4):
        greet += [p_peer(0, d)[1], s_peer(0, d)[1]]
    for to in greet:
        pl.semaphore_signal(barrier, inc=1, device_id=to, device_id_type=MESH)
    pl.semaphore_wait(barrier, len(greet))

    swaps = []
    for h in range(2):
        swaps.append(
            (
                q_hbm.at[:, cut(oh * 2048 + h * 1024, 1024)],
                q.at[h, place[h][0], place[h][1], cut(yh * ROWS, ROWS)],
            )
        )
    swaps.append((nk_hbm.at[:, cut(oh * HD, HD)], nkd.at[cut(yh * ROWS, ROWS), pl.ds(0, HD)]))
    swaps.append((nv_hbm.at[:, cut(oh * HD, HD)], nvd.at[cut(yh * ROWS, ROWS), pl.ds(0, HD)]))
    swaps.append((lens.at[0], lens.at[1]))
    swaps.append((ck_hbm.at[:, cut(oh * HD, HD)], kd.at[1, :, pl.ds(0, HD)]))
    swaps.append((cv_hbm.at[:, cut(oh * HD, HD)], vd.at[1, :, pl.ds(0, HD)]))
    swaps.append((w_hbm.at[cut(oh * 2048, 2048)], w.at[yh]))
    swap = [remote(a, b, ex_s.at[i], ex_r.at[i], partner) for i, (a, b) in enumerate(swaps)]
    for copy in swap[:7]:
        copy.start()

    mine[4].wait()
    mine[5].wait()
    swap[0].wait_recv()
    swap[1].wait_recv()

    def q_first(i):
        for h in range(2):
            ref = q.at[h, place[h][0], place[h][1], :, pl.ds(i * PIECE, PIECE)]
            for d in range(1, 4):
                remote(ref, ref, qa_s.at[0, h, i], qa_r.at[0, h, i], p_peer(h, d)[1]).start()

    def q_second(i):
        for h in range(2):
            await_bytes(q.at[h, pl.ds(0, 3), 0, :, pl.ds(i * PIECE, PIECE)], qa_r.at[0, h, i])
            ref = q.at[h, :, place[h][1], :, pl.ds(i * PIECE, PIECE)]
            for d in range(1, 4):
                remote(ref, ref, qa_s.at[1, h, i], qa_r.at[1, h, i], s_peer(h, d)[1]).start()

    def q_done(h, i):
        await_bytes(q.at[h, :, pl.ds(0, 3), :, cut(i * PIECE, PIECE)], qa_r.at[1, h, i])

    for i in range(PIECES):
        q_first(i)
    for i in range(PIECES):
        q_second(i)

    def settle(b):
        length = lens[b, 0:1, :]
        key0 = jnp.broadcast_to(kd[b, 0:1, :HD].astype(F32), (256, HD))

        def some(i, _):
            rows = cut(i * 256, 256)
            live = lax.broadcasted_iota(jnp.int32, (256, HD), 0) + i * 256 < length
            keys = jnp.where(live, kd[b, rows, :HD].astype(F32), key0).astype(BF16)
            kd[b, rows, :HD] = keys
            kd[b, rows, HD:] = keys
            vd[b, rows, :HD] = jnp.where(live, vd[b, rows, :HD].astype(F32), 0.0).astype(BF16)
            vd[b, rows, HD:] = jnp.where(live, 1.0, 0.0).astype(BF16)
            return 0

        lax.fori_loop(0, SLOTS // 256, some, 0)

    for copy in mine[:4]:
        copy.wait()
    settle(0)
    swap[2].wait_recv()
    swap[3].wait_recv()
    nkd[:32, HD:] = nkd[:32, :HD]
    nvd[:, HD:] = jnp.ones((HD, HD), BF16)
    row = lax.broadcasted_iota(jnp.int32, (TOK, HD), 0)
    lane = lax.broadcasted_iota(jnp.int32, (TOK, HD), 1)
    key_at = ((x * 2 + lane // ROWS) * NZ + z) * ROWS + lane % ROWS
    for h in range(2):
        first, second = row // 128, (row // 32) % 4
        xs, zs = (first, second) if h == 0 else (second, first)
        token = ((xs * 2 + (row // ROWS) % 2) * NZ + zs) * ROWS + row % ROWS
        bias[h] = jnp.where(jnp.logical_and(lane < 32, key_at <= token), 0.0, NEG)

    S, SN, M = (s0, s1), (sn0, sn1), (m0, m1)

    def step(b, score, weigh):
        if score is not None:
            c, h = score
            tile = q[h, :, :, :, cut(c * HD, HD)].reshape(TOK, HD).astype(F32) * SCALE
            high = tile.astype(BF16)
            low = (tile - high.astype(F32)).astype(BF16)
            query = jnp.concatenate([high, low], axis=1)
            if b == 0:
                fresh = (
                    lax.dot_general(query, nkd[...], (((1,), (1,)), ((), ())), preferred_element_type=F32)
                    + bias[h]
                )
                SN[h][...] = fresh
                peak = fresh
            else:
                peak = mx1[c, h]
        if weigh is not None:
            cw, hw = weigh
            top = M[hw][...]
            wide = jnp.tile(top, (1, SUB // HD))
            if b == 0:
                total = jnp.dot(
                    jnp.exp2(SN[hw][...] - top).astype(BF16), nvd[...], preferred_element_type=F32
                )
            else:
                fade = jnp.exp2(mx1[cw, hw] - top)
                total = o1[cw, hw] * jnp.concatenate([fade, fade], axis=1)
        for j in range(SLOTS // SUB):
            keys = slice(j * SUB, (j + 1) * SUB)
            if score is not None:
                block = lax.dot_general(
                    query, kd[b, keys, :], (((1,), (1,)), ((), ())), preferred_element_type=F32
                )
                S[h][:, keys] = block
                for t in range(SUB // HD):
                    peak = jnp.maximum(peak, block[:, t * HD : (t + 1) * HD])
            if weigh is not None:
                probs = jnp.exp2(S[hw][:, keys] - wide).astype(BF16)
                total = total + jnp.dot(probs, vd[b, keys, :], preferred_element_type=F32)
        if score is not None:
            M[h][...] = jnp.broadcast_to(jnp.max(peak, axis=1, keepdims=True), (TOK, HD))
        if weigh is None:
            return
        if b == 0:
            o1[cw, hw] = total
            mx1[cw, hw] = top
        else:
            weight = total[:, HD:]
            part[hw, cw] = (total[:, :HD] / weight).astype(BF16)
            lts[hw, cw] = (top + jnp.log(weight) * LOG2E).T[0:8, :]
            for d in range(1, 4):
                to, who = p_peer(hw, d)
                remote(
                    part.at[hw, cw, cut(to * 128, 128)], r1o.at[hw, cw, d - 1],
                    rs_s.at[0, hw, cw], rs_r.at[0, hw, cw], who,
                ).start()
                remote(
                    lts.at[hw, cw, :, cut(to * 128, 128)], r1l.at[hw, cw, d - 1],
                    rl_s.at[0, hw, cw], rl_r.at[0, hw, cw], who,
                ).start()

    def spread(line):
        return jnp.broadcast_to(line, (HD, HD)).T

    def join(parts, logs):
        top = jnp.maximum(jnp.maximum(logs[0], logs[1]), jnp.maximum(logs[2], logs[3]))
        weights = [jnp.exp2(v - top) for v in logs]
        total = weights[0] + weights[1] + weights[2] + weights[3]
        summed = weights[0] * parts[0].astype(F32)
        for i in range(1, 4):
            summed = summed + weights[i] * parts[i].astype(F32)
        return (summed / total).astype(BF16), top, total

    def serve_1(h, c):
        await_bytes(r1o.at[h, c], rs_r.at[0, h, c])
        await_bytes(r1l.at[h, c], rl_r.at[0, h, c])
        p, s = place[h]
        logs = [spread(lts[h, c, 0:1, cut(p * 128, 128)])]
        parts = [part[h, c, cut(p * 128, 128), :]]
        for i in range(3):
            logs.append(spread(r1l[h, c, i, 0:1, :]))
            parts.append(r1o[h, c, i])
        joined, top, total = join(parts, logs)
        s2o[h, c] = joined
        s2l[h, c] = (top + jnp.log(total) * LOG2E).T[0:8, :]
        for d in range(1, 4):
            to, who = s_peer(h, d)
            remote(
                s2o.at[h, c, cut(to * 32, 32)], r2o.at[h, c, d - 1],
                rs_s.at[1, h, c], rs_r.at[1, h, c], who,
            ).start()
            remote(
                s2l.at[h, c], r2l.at[h, c, d - 1], rl_s.at[1, h, c], rl_r.at[1, h, c], who
            ).start()

    def serve_2(h, c):
        await_bytes(r2o.at[h, c], rs_r.at[1, h, c])
        await_bytes(r2l.at[h, c], rl_r.at[1, h, c])
        p, s = place[h]
        tmp[0] = spread(s2l[h, c, 0:1, :])
        parts = [s2o[h, c, cut(s * 32, 32), :]]
        for i in range(3):
            tmp[i + 1] = spread(r2l[h, c, i, 0:1, :])
            parts.append(r2o[h, c, i])
        logs = [tmp[i, cut(s * 32, 32), :] for i in range(4)]
        joined, _, _ = join(parts, logs)
        g[h, p, s, :, cut(c * HD, HD)] = joined
        ref = g.at[h, p, s, :, cut(c * HD, HD)]
        for d in range(1, 4):
            remote(ref, ref, ag_s.at[0, h, c], ag_r.at[0, h, c], s_peer(h, d)[1]).start()

    def serve_3(h, c):
        p, s = place[h]
        await_bytes(g.at[h, p, pl.ds(0, 3), :, cut(c * HD, HD)], ag_r.at[0, h, c])
        ref = g.at[h, p, :, :, cut(c * HD, HD)]
        for d in range(1, 4):
            remote(ref, ref, ag_s.at[1, h, c], ag_r.at[1, h, c], p_peer(h, d)[1]).start()

    def serve_4(h, c):
        await_bytes(g.at[h, pl.ds(0, 3), :, :, cut(c * HD, HD)], ag_r.at[1, h, c])

    def serve(c, last):
        for k, act in ((1, serve_1), (2, serve_2), (3, serve_3), (4, serve_4)):
            def run(act=act, k=k):
                for h in range(2):
                    act(h, c - k)
            ok = c - k < HEADS if last else c >= k
            pl.when(ok)(run)

    for h in range(2):
        q_done(h, 0)
    step(0, (0, 0), None)

    def own(c, _):
        step(0, (c, 1), (c, 0))
        ahead = jnp.minimum(c + 1, HEADS - 1)

        @pl.when(jnp.logical_and(lax.rem(c, 2) == 1, c < HEADS - 1))
        def _():
            for h in range(2):
                q_done(h, (c + 1) // 2)

        step(0, (ahead, 0), (c, 1))
        return 0

    lax.fori_loop(0, HEADS, own, 0)

    for i in (4, 5, 6):
        swap[i].wait_recv()
    swap[7].start()
    settle(1)
    step(1, (0, 0), None)

    def other(c, _):
        step(1, (c, 1), (c, 0))
        step(1, (jnp.minimum(c + 1, HEADS - 1), 0), (c, 1))
        serve(c, False)
        return 0

    lax.fori_loop(0, HEADS, other, 0)

    def drain(c, _):
        serve(c, True)
        return 0

    lax.fori_loop(HEADS, HEADS + 4, drain, 0)

    own_w.wait()
    swap[7].wait_recv()

    def project(cc, put):
        blocks = []
        for ll in range(2):
            t = ll * 2 + cc
            blocks.append(
                jnp.concatenate(
                    [g[0, t].reshape(128, 1024), g[1, :, t].reshape(128, 1024)], axis=1
                )
            )
        heads = jnp.concatenate(blocks, axis=0)
        for k in range(2):
            res = jnp.dot(heads, w[k], preferred_element_type=F32)
            for ll in range(2):
                put(ll, k, res[ll * 128 : (ll + 1) * 128])

    def put_sent(ll, k, res):
        es1[ll, k] = res.astype(BF16)

    def put_kept(ll, k, res):
        acc[ll, k] = res

    project(1 - core, put_sent)
    to_core = remote(es1, er1, e_s.at[0], e_r.at[0], sibling)
    to_core.start()
    project(core, put_kept)
    to_core.wait_recv()
    last = []
    for i, (dl, dk) in enumerate(((1, 0), (0, 1), (1, 1))):
        ll = lax.rem(yl + dl, 2)
        k = lax.rem(yh + dk, 2)
        es2[i] = (acc[ll, k] + er1[ll, k].astype(F32)).astype(BF16)
        copy = remote(es2.at[i], er2.at[i], e_s.at[1 + i], e_r.at[1 + i], ends[i])
        copy.start()
        last.append(copy)
    result = acc[yl, yh] + er1[yl, yh].astype(F32)
    for i in range(3):
        last[i].wait_recv()
        result = result + er2[i].astype(F32)
    result = result.astype(BF16)
    for hh in range(2):
        for zz in range(NZ):
            a, b = (zz * 2 + hh) * ROWS, (hh * NZ + zz) * ROWS
            out_ref[b : b + ROWS, :] = result[a : a + ROWS]

    to_core.wait_send()
    for copy in last + swap:
        copy.wait_send()
    for h in range(2):
        for i in range(PIECES):
            cols = pl.ds(i * PIECE, PIECE)
            await_bytes(q.at[h, pl.ds(0, 3), 0, :, cols], qa_s.at[0, h, i])
            await_bytes(q.at[h, :, pl.ds(0, 3), :, cols], qa_s.at[1, h, i])

    def sent(c, _):
        cols = cut(c * HD, HD)
        for h in range(2):
            await_bytes(r1o.at[h, c], rs_s.at[0, h, c])
            await_bytes(r1l.at[h, c], rl_s.at[0, h, c])
            await_bytes(r2o.at[h, c], rs_s.at[1, h, c])
            await_bytes(r2l.at[h, c], rl_s.at[1, h, c])
            await_bytes(g.at[h, 0, pl.ds(0, 3), :, cols], ag_s.at[0, h, c])
            await_bytes(g.at[h, pl.ds(0, 3), :, :, cols], ag_s.at[1, h, c])
        return 0

    lax.fori_loop(0, HEADS, sent, 0)


def body(queries, new_keys, new_values, cache_keys, cache_values, cache_lens, out_weight):
    V = pltpu.VMEM
    D = pltpu.SemaphoreType.DMA
    any_ = pl.BlockSpec(memory_space=pl.ANY)
    return pl.pallas_call(
        kernel,
        out_shape=jax.ShapeDtypeStruct((128, 512), BF16),
        in_specs=[any_, any_, any_, any_, any_, pl.BlockSpec(memory_space=pltpu.SMEM), any_],
        out_specs=pl.BlockSpec(memory_space=pltpu.VMEM),
        scratch_shapes=[
            V((2, 4, 4, 32, 1024), BF16),
            V((2, SLOTS, 2 * HD), BF16),
            V((2, SLOTS, 2 * HD), BF16),
            V((HD, 2 * HD), BF16),
            V((HD, 2 * HD), BF16),
            V((2, 8, HD), jnp.int32),
            V((2, TOK, HD), F32),
            V((TOK, SLOTS), F32),
            V((TOK, SLOTS), F32),
            V((TOK, HD), F32),
            V((TOK, HD), F32),
            V((TOK, HD), F32),
            V((TOK, HD), F32),
            V((HEADS, 2, TOK, 2 * HD), F32),
            V((HEADS, 2, TOK, HD), F32),
            V((2, HEADS, TOK, HD), BF16),
            V((2, HEADS, 8, TOK), F32),
            V((2, HEADS, 3, 128, HD), BF16),
            V((2, HEADS, 3, 8, 128), F32),
            V((2, HEADS, 128, HD), BF16),
            V((2, HEADS, 8, 128), F32),
            V((2, HEADS, 3, 32, HD), BF16),
            V((2, HEADS, 3, 8, 128), F32),
            V((4, 128, HD), F32),
            V((2, 4, 4, 32, 1024), BF16),
            V((2, 2048, 512), BF16),
            V((2, 2, 128, 512), F32),
            V((2, 2, 128, 512), BF16),
            V((2, 2, 128, 512), BF16),
            V((3, 128, 512), BF16),
            V((3, 128, 512), BF16),
            D((7,)),
            D((8,)),
            D((8,)),
            D((2, 2, PIECES)),
            D((2, 2, PIECES)),
            D((2, 2, HEADS)),
            D((2, 2, HEADS)),
            D((2, 2, HEADS)),
            D((2, 2, HEADS)),
            D((2, 2, HEADS)),
            D((2, 2, HEADS)),
            D((4,)),
            D((4,)),
        ],
        compiler_params=pltpu.CompilerParams(
            collective_id=0, has_side_effects=True, vmem_limit_bytes=60 << 20
        ),
        cost_estimate=pl.CostEstimate(flops=20 << 30, bytes_accessed=16 << 20, transcendentals=40 << 20),
    )(queries, new_keys, new_values, cache_keys, cache_values, cache_lens, out_weight)


def solution(mesh):
    in_specs = (
        P("ctx", "tp"),
        P("ctx", "tp"),
        P("ctx", "tp"),
        P("ctx", "tp"),
        P("ctx", "tp"),
        P("ctx"),
        P("tp", "ctx"),
    )
    return jax.shard_map(body, mesh=mesh, in_specs=in_specs, out_specs=P("tp", "ctx"), check_vma=False)
```

```python
import math

import jax
import jax.numpy as jnp
from jax import lax
from jax.experimental import pallas as pl
from jax.experimental.pallas import tpu as pltpu
from jax.sharding import PartitionSpec as P

HD = 128
NX = 4
NZ = 4
ROWS = 16
SLOTS = 2048
HEADS = 8
TOK = NX * NZ * 2 * ROWS
PIECES = 4
PIECE = HEADS // PIECES * HD
FIRST = ((0, PIECE), (PIECE, 1024 - PIECE), (1024, HD))
SECOND = tuple((i * PIECE, PIECE) for i in range(PIECES)) + ((1024, HD),)
LAGS = (3, 7, 11)
EARLY = 6
SUB = 512
NEG = -1e30
LOG2E = 1.4426950408889634
SCALE = LOG2E / math.sqrt(HD)
F32 = jnp.float32
BF16 = jnp.bfloat16
MESH = pl.DeviceIdType.MESH


def kernel(
    q_hbm, nk_hbm, nv_hbm, ck_hbm, cv_hbm, len_ref, w_hbm, out_ref,
    q, kd, vd, lens, s0, s1, m0, m1, oa, ob, xa, xb, ofa, ofb, mfa, mfb, fo, fl,
    part, lts, r1o, r1l, s2o, s2l, r2o, r2l, tmp, g, w,
    acc, es1, er1, es2, er2,
    loc, ex_s, ex_r, qn_s, qn_r, qf_s, qf_r, qa_s, qa_r,
    rs_s, rs_r, rl_s, rl_r, ag_s, ag_r, c_s, c_r, e_s, e_r,
):
    ctx = lax.axis_index("ctx")
    tp = lax.axis_index("tp")
    z = lax.rem(ctx, NZ)
    yh = lax.rem(ctx // NZ, 2)
    x = ctx // (2 * NZ)
    core = lax.rem(tp, 2)
    yl = tp // 2
    oh = 1 - yh

    def at(xx, hh, zz, ll, cc):
        return ((xx * 2 + hh) * NZ + zz, ll * 2 + cc)

    partner = at(x, oh, z, yl, core)
    sibling = at(x, yh, z, yl, 1 - core)
    place = ((x, z), (z, x))

    def p_peer(h, d, hh=yh):
        to = lax.rem(place[h][0] + d, 4)
        return to, (at(to, hh, z, yl, core) if h == 0 else at(x, hh, to, yl, core))

    def s_peer(h, d):
        to = lax.rem(place[h][1] + d, 4)
        return to, (at(x, yh, to, yl, core) if h == 0 else at(to, yh, z, yl, core))

    ends = [at(x, oh, z, yl, core), at(x, oh, z, 1 - yl, core), at(x, yh, z, 1 - yl, core)]

    def local(src, dst, sem):
        return pltpu.make_async_copy(src, dst, sem)

    def remote(src, dst, ssem, rsem, to):
        return pltpu.make_async_remote_copy(
            src_ref=src, dst_ref=dst, send_sem=ssem, recv_sem=rsem, device_id=to, device_id_type=MESH
        )

    def await_bytes(ref, sem):
        pltpu.make_async_copy(ref, ref, sem).wait()

    def cut(start, size):
        return pl.ds(pl.multiple_of(start, size), size)

    news = (nk_hbm, nv_hbm)
    mine = [
        local(ck_hbm.at[:, cut(yh * HD, HD)], kd.at[0, :, pl.ds(0, HD)], loc.at[0]),
        local(cv_hbm.at[:, cut(yh * HD, HD)], vd.at[0, :, pl.ds(0, HD)], loc.at[1]),
    ]
    for h in range(2):
        own_q = q.at[h, place[h][0], place[h][1], cut(yh * ROWS, ROWS)]
        mine.append(
            local(q_hbm.at[:, cut(yh * 2048 + h * 1024, 1024)], own_q.at[:, pl.ds(0, 1024)], loc.at[2 + h])
        )
        mine.append(
            local(news[h].at[:, cut(yh * HD, HD)], own_q.at[:, pl.ds(1024, HD)], loc.at[4 + h])
        )
    own_w = local(w_hbm.at[cut(yh * 2048, 2048)], w.at[yh], loc.at[6])
    for copy in mine:
        copy.start()
    own_w.start()

    barrier = pltpu.get_barrier_semaphore()
    greet = [sibling] + ends
    for d in range(1, 4):
        for h in range(2):
            greet += [p_peer(h, d)[1], p_peer(h, d, oh)[1]]
    for to in greet:
        pl.semaphore_signal(barrier, inc=1, device_id=to, device_id_type=MESH)
    lens[0] = jnp.broadcast_to(len_ref[0], (8, HD))

    fo[...] = jnp.zeros((2, HEADS, HD, HD), BF16)
    pl.semaphore_wait(barrier, len(greet))

    def q_first(i):
        start, size = FIRST[i]
        for d in (2, 1, 3, 0):
            for h in range(2):
                dst = q.at[h, place[h][0], place[h][1], cut(yh * ROWS, ROWS), pl.ds(start, size)]
                for far, hh, ss, rs in ((1, oh, qf_s, qf_r), (0, yh, qn_s, qn_r)):
                    if d == 0 and not far:
                        continue
                    if i < 2:
                        src = q_hbm.at[:, pl.ds(pl.multiple_of(hh * 2048 + h * 1024 + start, 256), size)]
                    else:
                        src = news[h].at[:, cut(hh * HD, HD)]
                    remote(src, dst, ss.at[h, i], rs.at[h, i], p_peer(h, d, hh)[1]).start()

    def q_second(i):
        start, size = SECOND[i]
        for d in (2, 1, 3):
            for h in range(2):
                ref = q.at[h, :, place[h][1], :, pl.ds(start, size)]
                remote(ref, ref, qa_s.at[h, i], qa_r.at[h, i], s_peer(h, d)[1]).start()

    def q_lines(i, sems):
        start, size = FIRST[i]
        for h in range(2):
            await_bytes(q.at[h, pl.ds(0, 3), 0, pl.ds(0, ROWS), pl.ds(start, size)], sems[0].at[h, i])
            await_bytes(q.at[h, :, 0, pl.ds(0, ROWS), pl.ds(start, size)], sems[1].at[h, i])

    def q_done(h, i):
        await_bytes(q.at[h, :, pl.ds(0, 3), :, cut(i * PIECE, PIECE)], qa_r.at[h, i])

    for i in range(3):
        q_first(i)

    swaps = (
        (lens.at[0], lens.at[1]),
        (ck_hbm.at[:, cut(oh * HD, HD)], kd.at[1, :, pl.ds(0, HD)]),
        (cv_hbm.at[:, cut(oh * HD, HD)], vd.at[1, :, pl.ds(0, HD)]),
        (w_hbm.at[cut(oh * 2048, 2048)], w.at[yh]),
    )
    swap = [remote(a, b, ex_s.at[i], ex_r.at[i], partner) for i, (a, b) in enumerate(swaps)]
    for copy in swap[:3]:
        copy.start()

    def settle(b):
        length = lens[b, 0:1, :]
        key0 = jnp.broadcast_to(kd[b, 0:1, :HD].astype(F32), (256, HD))

        def some(i, _):
            rows = cut(i * 256, 256)
            live = lax.broadcasted_iota(jnp.int32, (256, HD), 0) + i * 256 < length
            keys = jnp.where(live, kd[b, rows, :HD].astype(F32), key0).astype(BF16)
            kd[b, rows, :HD] = keys
            kd[b, rows, HD:] = keys
            vd[b, rows, :HD] = jnp.where(live, vd[b, rows, :HD].astype(F32), 0.0).astype(BF16)
            vd[b, rows, HD:] = jnp.where(live, 1.0, 0.0).astype(BF16)
            return 0

        lax.fori_loop(0, SLOTS // 256, some, 0)

    for copy in mine:
        copy.wait()
    settle(0)

    q_lines(0, (qn_r, qf_r))
    q_second(0)
    q_lines(1, (qn_r, qf_r))
    for i in range(1, PIECES):
        q_second(i)
    q_lines(2, (qn_r, qf_r))
    q_second(PIECES)

    S, M = (s0, s1), (m0, m1)
    O, MX, OF, MF = (oa, ob), (xa, xb), (ofa, ofb), (mfa, mfb)

    def split(tile):
        tile = tile.astype(F32) * SCALE
        high = tile.astype(BF16)
        low = (tile - high.astype(F32)).astype(BF16)
        return jnp.concatenate([high, low], axis=1)

    def step(score, weigh):
        if score is not None:
            c, b, h = score
            query = split(q[h, :, :, :, cut(c * HD, HD)].reshape(TOK, HD))
            peak = MX[h][c] if b else None
        if weigh is not None:
            cw, bw, hw = weigh
            top = M[hw][...]
            wide = jnp.tile(top, (1, SUB // HD))
            total = None
            if bw:
                fade = jnp.exp2(MX[hw][cw] - top)
                total = O[hw][cw] * jnp.concatenate([fade, fade], axis=1)
        for j in range(SLOTS // SUB):
            keys = slice(j * SUB, (j + 1) * SUB)
            if score is not None:
                block = lax.dot_general(
                    query, kd[b, keys, :], (((1,), (1,)), ((), ())), preferred_element_type=F32
                )
                S[h][:, keys] = block
                for t in range(SUB // HD):
                    part_of = block[:, t * HD : (t + 1) * HD]
                    peak = part_of if peak is None else jnp.maximum(peak, part_of)
            if weigh is not None:
                probs = jnp.exp2(S[hw][:, keys] - wide).astype(BF16)
                term = jnp.dot(probs, vd[bw, keys, :], preferred_element_type=F32)
                total = term if total is None else total + term
        if score is not None:
            M[h][...] = jnp.broadcast_to(jnp.max(peak, axis=1, keepdims=True), (TOK, HD))
        if weigh is not None:
            if bw:
                OF[hw][...] = total
                MF[hw][...] = top
            else:
                O[hw][cw] = total
                MX[hw][cw] = top

    def finish(h, c):
        weight = OF[h][:, HD:]
        part[h, c] = (OF[h][:, :HD] / weight).astype(BF16)
        lts[h, c] = (MF[h][...] + jnp.log(weight) * LOG2E).T[0:1, :]
        for d in (2, 1, 3):
            to, who = p_peer(h, d)
            remote(
                part.at[h, c, cut(to * 128, 128)], r1o.at[h, c, d - 1],
                rs_s.at[0, h, c], rs_r.at[0, h, c], who,
            ).start()
            remote(
                lts.at[h, c, :, cut(to * 128, 128)], r1l.at[h, c, d - 1],
                rl_s.at[0, h, c], rl_r.at[0, h, c], who,
            ).start()

    def spread(line):
        return jnp.broadcast_to(line, (HD, HD)).T

    def balance(logs):
        top = logs[0]
        for v in logs[1:]:
            top = jnp.maximum(top, v)
        weights = [jnp.exp2(v - top) for v in logs]
        total = weights[0]
        for v in weights[1:]:
            total = total + v
        return [v / total for v in weights], top + jnp.log(total) * LOG2E

    def join(parts, shares):
        summed = shares[0] * parts[0].astype(F32)
        for a, v in zip(parts[1:], shares[1:]):
            summed = summed + v * a.astype(F32)
        return summed.astype(BF16)

    def serve_1(h, c):
        await_bytes(r1o.at[h, c], rs_r.at[0, h, c])
        await_bytes(r1l.at[h, c], rl_r.at[0, h, c])
        p, s = place[h]
        shares, logs = balance(
            [lts[h, c, :, cut(p * 128, 128)]] + [r1l[h, c, i] for i in range(3)] + [fl[h, c]]
        )
        s2l[h, c] = logs
        s2o[h, c] = join(
            [part[h, c, cut(p * 128, 128), :]] + [r1o[h, c, i] for i in range(3)] + [fo[h, c]],
            [spread(v) for v in shares],
        )
        for d in (2, 1, 3):
            who = s_peer(h, d)[1]
            remote(
                s2o.at[h, c], r2o.at[h, c, d - 1], rs_s.at[1, h, c], rs_r.at[1, h, c], who
            ).start()
            remote(
                s2l.at[h, c], r2l.at[h, c, d - 1], rl_s.at[1, h, c], rl_r.at[1, h, c], who
            ).start()

    def serve_2(h, c):
        await_bytes(r2o.at[h, c], rs_r.at[1, h, c])
        await_bytes(r2l.at[h, c], rl_r.at[1, h, c])
        p, s = place[h]
        shares, _ = balance([s2l[h, c]] + [r2l[h, c, i] for i in range(3)])
        joined = join(
            [s2o[h, c]] + [r2o[h, c, i] for i in range(3)], [spread(v) for v in shares]
        )
        ref = g.at[h, p, :, :, cut(c * HD, HD)]
        g[h, p, :, :, cut(c * HD, HD)] = joined.reshape(4, 32, HD)
        for d in (2, 1, 3):
            remote(ref, ref, ag_s.at[h, c], ag_r.at[h, c], p_peer(h, d)[1]).start()

    def serve_3(h, c):
        await_bytes(g.at[h, pl.ds(0, 3), :, :, cut(c * HD, HD)], ag_r.at[h, c])

    def fresh():
        keys = q[0, :, :, :, 1024:].reshape(TOK, HD)
        keys = jnp.concatenate([keys, keys], axis=1)
        values = jnp.concatenate(
            [q[1, zz, xx, :, 1024:] for xx in range(NX) for zz in range(NZ)], axis=0
        )
        values = jnp.concatenate([values, jnp.ones((TOK, HD), BF16)], axis=1)
        rows = []
        for h in range(2):
            for c in range(HEADS):
                rows.append(q[h, place[h][0], place[h][1], :, c * HD : (c + 1) * HD])
        query = split(jnp.concatenate(rows, axis=0))
        row = lax.broadcasted_iota(jnp.int32, (TOK, TOK), 0)
        lane = lax.broadcasted_iota(jnp.int32, (TOK, TOK), 1)
        token = ((x * 2 + (row // ROWS) % 2) * NZ + z) * ROWS + row % ROWS
        key_at = ((lane // 128 * 2 + (lane // ROWS) % 2) * NZ + (lane // 32) % 4) * ROWS + lane % ROWS
        score = lax.dot_general(query, keys, (((1,), (1,)), ((), ())), preferred_element_type=F32)
        score = jnp.where(key_at <= token, score, NEG)
        top = jnp.broadcast_to(jnp.max(score, axis=1, keepdims=True), (TOK, HD))
        probs = jnp.exp2(score - jnp.tile(top, (1, TOK // HD))).astype(BF16)
        total = jnp.dot(probs, values, preferred_element_type=F32)
        weight = total[:, HD:]
        part_of = (total[:, :HD] / weight).astype(BF16).reshape(2, HEADS, 32, HD)
        logs = (top + jnp.log(weight) * LOG2E).reshape(2, HEADS, 32, HD)
        for h in range(2):
            mine_32 = cut(place[h][1] * 32, 32)
            tmp[...] = jnp.full((HD, HD), NEG, F32)
            for c in range(HEADS):
                fo[h, c, mine_32, :] = part_of[h, c]
                tmp[mine_32, :] = logs[h, c]
                fl[h, c] = tmp[...].T[0:1, :]

    def serve(c, half):
        for lag, act in ((LAGS[2], serve_3), (LAGS[1], serve_2), (LAGS[0], serve_1)):
            h = (half - lag) % 2
            j = c - (lag + h - half) // 2

            @pl.when(jnp.logical_and(j >= 0, j < HEADS))
            def _(act=act, j=j, h=h):
                act(h, j)

    for h in range(2):
        q_done(h, 0)
    step((0, 0, 0), None)

    def own(c, _):
        step((c, 0, 1), (c, 0, 0))

        @pl.when(lax.rem(c, 2) == 1)
        def _():
            for h in range(2):
                q_done(h, (c + 1) // 2)

        step((c + 1, 0, 0), (c, 0, 1))
        return 0

    LAST = HEADS - 1
    lax.fori_loop(0, LAST, own, 0)
    step((LAST, 0, 1), (LAST, 0, 0))
    for h in range(2):
        await_bytes(q.at[h, :, pl.ds(0, 3), :, pl.ds(1024, HD)], qa_r.at[h, PIECES])
    fresh()

    for copy in swap[:3]:
        copy.wait_recv()
    swap[3].start()
    settle(1)
    step((0, 1, 0), (LAST, 0, 1))
    step((0, 1, 1), (0, 1, 0))

    def other(c, _):
        finish(0, c)
        step((c + 1, 1, 0), (c, 1, 1))
        serve(c, 0)
        finish(1, c)
        step((c + 1, 1, 1), (c + 1, 1, 0))
        serve(c, 1)
        return 0

    lax.fori_loop(0, LAST, other, 0)
    finish(0, LAST)
    step(None, (LAST, 1, 1))
    finish(1, LAST)

    def drain(c, _):
        serve(c, 0)
        serve(c, 1)
        return 0

    BREAK = (2 * HEADS - 1 + LAGS[1]) // 2 + 1
    lax.fori_loop(LAST, BREAK, drain, 0)

    def heads_of(cc, first, count):
        blocks = []
        cols = pl.ds(first * HD, count * HD)
        for ll in range(2):
            t = ll * 2 + cc
            blocks.append(
                jnp.concatenate(
                    [
                        g[0, t, :, :, cols].reshape(128, count * HD),
                        g[1, :, t, :, cols].reshape(128, count * HD),
                    ],
                    axis=1,
                )
            )
        return jnp.concatenate(blocks, axis=0)

    def project(heads, k, first, count):
        size = count * HD
        top = jnp.dot(heads[:, :size], w[k, pl.ds(first * HD, size)], preferred_element_type=F32)
        return top + jnp.dot(
            heads[:, size:], w[k, pl.ds(1024 + first * HD, size)], preferred_element_type=F32
        )

    own_w.wait()
    for k in (yh, oh):
        if k is oh:
            swap[3].wait_recv()
        for a, cc in enumerate((1 - core, core)):
            acc[a, k] = project(heads_of(cc, 0, EARLY), k, 0, EARLY)

    lax.fori_loop(BREAK, (2 * HEADS - 1 + LAGS[2]) // 2 + 1, drain, 0)

    to_core = []
    late = HEADS - EARLY
    for k in (oh, yh):
        es1[k] = (acc[0, k] + project(heads_of(1 - core, EARLY, late), k, EARLY, late)).astype(BF16)
        copy = remote(es1.at[k], er1.at[k], c_s.at[k], c_r.at[k], sibling)
        copy.start()
        to_core.append(copy)
    for k in (oh, yh):
        acc[1, k] += project(heads_of(core, EARLY, late), k, EARLY, late)
    last = []

    def send(i, ll, k):
        rows = cut(ll * 128, 128)
        es2[i] = (acc[1, k, rows, :] + er1[k, rows, :].astype(F32)).astype(BF16)
        copy = remote(es2.at[i], er2.at[i], e_s.at[i], e_r.at[i], ends[i])
        copy.start()
        last.append(copy)

    to_core[0].wait_recv()
    send(0, yl, oh)
    send(1, 1 - yl, oh)
    to_core[1].wait_recv()
    send(2, 1 - yl, yh)
    rows = cut(yl * 128, 128)
    result = acc[1, yh, rows, :] + er1[yh, rows, :].astype(F32)
    for i in (2, 1, 0):
        last[i].wait_recv()
        result = result + er2[i].astype(F32)
    result = result.astype(BF16)
    for hh in range(2):
        for zz in range(NZ):
            a, b = (zz * 2 + hh) * ROWS, (hh * NZ + zz) * ROWS
            out_ref[b : b + ROWS, :] = result[a : a + ROWS]

    for copy in to_core + last + swap:
        copy.wait_send()
    for i in range(3):
        q_lines(i, (qn_s, qf_s))
    for h in range(2):
        for i in range(PIECES + 1):
            start, size = SECOND[i]
            await_bytes(q.at[h, :, pl.ds(0, 3), :, pl.ds(start, size)], qa_s.at[h, i])

    def sent(c, _):
        cols = cut(c * HD, HD)
        for h in range(2):
            await_bytes(r1o.at[h, c], rs_s.at[0, h, c])
            await_bytes(r1l.at[h, c], rl_s.at[0, h, c])
            await_bytes(r2o.at[h, c], rs_s.at[1, h, c])
            await_bytes(r2l.at[h, c], rl_s.at[1, h, c])
            await_bytes(g.at[h, pl.ds(0, 3), :, :, cols], ag_s.at[h, c])
        return 0

    lax.fori_loop(0, HEADS, sent, 0)


def body(queries, new_keys, new_values, cache_keys, cache_values, cache_lens, out_weight):
    V = pltpu.VMEM
    D = pltpu.SemaphoreType.DMA
    any_ = pl.BlockSpec(memory_space=pl.ANY)
    return pl.pallas_call(
        kernel,
        out_shape=jax.ShapeDtypeStruct((128, 512), BF16),
        in_specs=[any_, any_, any_, any_, any_, pl.BlockSpec(memory_space=pltpu.SMEM), any_],
        out_specs=pl.BlockSpec(memory_space=pltpu.VMEM),
        scratch_shapes=[
            V((2, 4, 4, 32, 1152), BF16),
            V((2, SLOTS, 2 * HD), BF16),
            V((2, SLOTS, 2 * HD), BF16),
            V((2, 8, HD), jnp.int32),
            V((TOK, SLOTS), F32),
            V((TOK, SLOTS), F32),
            V((TOK, HD), F32),
            V((TOK, HD), F32),
            V((HEADS, TOK, 2 * HD), F32),
            V((HEADS, TOK, 2 * HD), F32),
            V((HEADS, TOK, HD), F32),
            V((HEADS, TOK, HD), F32),
            V((TOK, 2 * HD), F32),
            V((TOK, 2 * HD), F32),
            V((TOK, HD), F32),
            V((TOK, HD), F32),
            V((2, HEADS, HD, HD), BF16),
            V((2, HEADS, 1, HD), F32),
            V((2, HEADS, TOK, HD), BF16),
            V((2, HEADS, 1, TOK), F32),
            V((2, HEADS, 3, 128, HD), BF16),
            V((2, HEADS, 3, 1, 128), F32),
            V((2, HEADS, 128, HD), BF16),
            V((2, HEADS, 1, 128), F32),
            V((2, HEADS, 3, 128, HD), BF16),
            V((2, HEADS, 3, 1, 128), F32),
            V((HD, HD), F32),
            V((2, 4, 4, 32, 1024), BF16),
            V((2, 2048, 512), BF16),
            V((2, 2, 256, 512), F32),
            V((2, 256, 512), BF16),
            V((2, 256, 512), BF16),
            V((3, 128, 512), BF16),
            V((3, 128, 512), BF16),
            D((7,)),
            D((4,)),
            D((4,)),
            D((2, 3)),
            D((2, 3)),
            D((2, 3)),
            D((2, 3)),
            D((2, PIECES + 1)),
            D((2, PIECES + 1)),
            D((2, 2, HEADS)),
            D((2, 2, HEADS)),
            D((2, 2, HEADS)),
            D((2, 2, HEADS)),
            D((2, HEADS)),
            D((2, HEADS)),
            D((2,)),
            D((2,)),
            D((3,)),
            D((3,)),
        ],
        compiler_params=pltpu.CompilerParams(
            collective_id=0, has_side_effects=True, vmem_limit_bytes=60 << 20
        ),
        cost_estimate=pl.CostEstimate(flops=20 << 30, bytes_accessed=16 << 20, transcendentals=40 << 20),
    )(queries, new_keys, new_values, cache_keys, cache_values, cache_lens, out_weight)


def solution(mesh):
    in_specs = (
        P("ctx", "tp"),
        P("ctx", "tp"),
        P("ctx", "tp"),
        P("ctx", "tp"),
        P("ctx", "tp"),
        P("ctx"),
        P("tp", "ctx"),
    )
    return jax.shard_map(body, mesh=mesh, in_specs=in_specs, out_specs=P("tp", "ctx"), check_vma=False)
```

```python
import math

import jax
import jax.numpy as jnp
from jax import lax
from jax.experimental import pallas as pl
from jax.experimental.pallas import tpu as pltpu
from jax.sharding import PartitionSpec as P

HD = 128
NX = 4
NZ = 4
ROWS = 16
SLOTS = 2048
HEADS = 8
TOK = NX * NZ * 2 * ROWS
PIECES = 8
PIECE = HEADS // PIECES * HD
FIRST = ((0, PIECE), (PIECE, 1024 - PIECE), (1024, HD))
SECOND = tuple((i * PIECE, PIECE) for i in range(PIECES)) + ((1024, HD),)
LAGS = (3, 7, 12)
EARLY = 6
SUB = 512
NEG = -1e30
LOG2E = 1.4426950408889634
SCALE = LOG2E / math.sqrt(HD)
F32 = jnp.float32
BF16 = jnp.bfloat16
MESH = pl.DeviceIdType.MESH


def kernel(
    q_hbm, nk_hbm, nv_hbm, ck_hbm, cv_hbm, len_ref, w_hbm, out_ref,
    q, kd, vd, lens, s0, s1, m0, m1, oa, ob, xa, xb, ofa, ofb, mfa, mfb, fo, fl,
    part, lts, r1o, r1l, s2o, s2l, r2o, r2l, tmp, g, w,
    acc, es1, er1, es2, er2,
    loc, ex_s, ex_r, qn_s, qn_r, qf_s, qf_r, qa_s, qa_r,
    rs_s, rs_r, rl_s, rl_r, ag_s, ag_r, c_s, c_r, e_s, e_r,
):
    ctx = lax.axis_index("ctx")
    tp = lax.axis_index("tp")
    z = lax.rem(ctx, NZ)
    yh = lax.rem(ctx // NZ, 2)
    x = ctx // (2 * NZ)
    core = lax.rem(tp, 2)
    yl = tp // 2
    oh = 1 - yh

    def at(xx, hh, zz, ll, cc):
        return ((xx * 2 + hh) * NZ + zz, ll * 2 + cc)

    partner = at(x, oh, z, yl, core)
    sibling = at(x, yh, z, yl, 1 - core)
    place = ((x, z), (z, x))

    def p_peer(h, d, hh=yh):
        to = lax.rem(place[h][0] + d, 4)
        return to, (at(to, hh, z, yl, core) if h == 0 else at(x, hh, to, yl, core))

    def s_peer(h, d):
        to = lax.rem(place[h][1] + d, 4)
        return to, (at(x, yh, to, yl, core) if h == 0 else at(to, yh, z, yl, core))

    ends = [at(x, oh, z, yl, core), at(x, oh, z, 1 - yl, core), at(x, yh, z, 1 - yl, core)]

    def local(src, dst, sem):
        return pltpu.make_async_copy(src, dst, sem)

    def remote(src, dst, ssem, rsem, to):
        return pltpu.make_async_remote_copy(
            src_ref=src, dst_ref=dst, send_sem=ssem, recv_sem=rsem, device_id=to, device_id_type=MESH
        )

    def await_bytes(ref, sem):
        pltpu.make_async_copy(ref, ref, sem).wait()

    def cut(start, size):
        return pl.ds(pl.multiple_of(start, size), size)

    news = (nk_hbm, nv_hbm)
    mine = [
        local(ck_hbm.at[:, cut(yh * HD, HD)], kd.at[0, :, pl.ds(0, HD)], loc.at[0]),
        local(cv_hbm.at[:, cut(yh * HD, HD)], vd.at[0, :, pl.ds(0, HD)], loc.at[1]),
    ]
    for h in range(2):
        own_q = q.at[h, place[h][0], place[h][1], cut(yh * ROWS, ROWS)]
        mine.append(
            local(q_hbm.at[:, cut(yh * 2048 + h * 1024, 1024)], own_q.at[:, pl.ds(0, 1024)], loc.at[2 + h])
        )
        mine.append(
            local(news[h].at[:, cut(yh * HD, HD)], own_q.at[:, pl.ds(1024, HD)], loc.at[4 + h])
        )
    own_w = local(w_hbm.at[cut(yh * 2048, 2048)], w.at[yh], loc.at[6])
    for copy in mine:
        copy.start()
    own_w.start()

    barrier = pltpu.get_barrier_semaphore()
    greet = [sibling] + ends
    for d in range(1, 4):
        for h in range(2):
            greet += [p_peer(h, d)[1], p_peer(h, d, oh)[1]]
    for to in greet:
        pl.semaphore_signal(barrier, inc=1, device_id=to, device_id_type=MESH)
    lens[0] = jnp.broadcast_to(len_ref[0], (8, HD))

    fo[...] = jnp.zeros((2, HEADS, HD, HD), BF16)
    pl.semaphore_wait(barrier, len(greet))

    def q_first(i):
        start, size = FIRST[i]
        for d in (2, 1, 3, 0):
            for h in range(2):
                dst = q.at[h, place[h][0], place[h][1], cut(yh * ROWS, ROWS), pl.ds(start, size)]
                for far, hh, ss, rs in ((1, oh, qf_s, qf_r), (0, yh, qn_s, qn_r)):
                    if d == 0 and not far:
                        continue
                    if i < 2:
                        src = q_hbm.at[:, pl.ds(pl.multiple_of(hh * 2048 + h * 1024 + start, HD), size)]
                    else:
                        src = news[h].at[:, cut(hh * HD, HD)]
                    remote(src, dst, ss.at[h, i], rs.at[h, i], p_peer(h, d, hh)[1]).start()

    def q_second(i):
        start, size = SECOND[i]
        for d in (2, 1, 3):
            for h in range(2):
                ref = q.at[h, :, place[h][1], :, pl.ds(start, size)]
                remote(ref, ref, qa_s.at[h, i], qa_r.at[h, i], s_peer(h, d)[1]).start()

    def q_lines(i, sems):
        start, size = FIRST[i]
        for h in range(2):
            await_bytes(q.at[h, pl.ds(0, 3), 0, pl.ds(0, ROWS), pl.ds(start, size)], sems[0].at[h, i])
            await_bytes(q.at[h, :, 0, pl.ds(0, ROWS), pl.ds(start, size)], sems[1].at[h, i])

    def q_done(h, i):
        await_bytes(q.at[h, :, pl.ds(0, 3), :, cut(i * PIECE, PIECE)], qa_r.at[h, i])

    for i in range(3):
        q_first(i)

    swaps = (
        (lens.at[0], lens.at[1]),
        (ck_hbm.at[:, cut(oh * HD, HD)], kd.at[1, :, pl.ds(0, HD)]),
        (cv_hbm.at[:, cut(oh * HD, HD)], vd.at[1, :, pl.ds(0, HD)]),
        (w_hbm.at[cut(oh * 2048, 2048)], w.at[yh]),
    )
    swap = [remote(a, b, ex_s.at[i], ex_r.at[i], partner) for i, (a, b) in enumerate(swaps)]
    def settle(b):
        length = lens[b, 0:1, :]
        key0 = jnp.broadcast_to(kd[b, 0:1, :HD].astype(F32), (256, HD))

        def some(i, _):
            rows = cut(i * 256, 256)
            live = lax.broadcasted_iota(jnp.int32, (256, HD), 0) + i * 256 < length
            keys = jnp.where(live, kd[b, rows, :HD].astype(F32), key0).astype(BF16)
            kd[b, rows, :HD] = keys
            kd[b, rows, HD:] = keys
            vd[b, rows, :HD] = jnp.where(live, vd[b, rows, :HD].astype(F32), 0.0).astype(BF16)
            vd[b, rows, HD:] = jnp.where(live, 1.0, 0.0).astype(BF16)
            return 0

        lax.fori_loop(0, SLOTS // 256, some, 0)

    for copy in mine:
        copy.wait()
    settle(0)

    q_lines(0, (qn_r, qf_r))
    q_second(0)
    q_lines(1, (qn_r, qf_r))
    for i in range(1, PIECES):
        q_second(i)
    for copy in swap[:3]:
        copy.start()

    S, M = (s0, s1), (m0, m1)
    O, MX, OF, MF = (oa, ob), (xa, xb), (ofa, ofb), (mfa, mfb)

    def split(tile):
        tile = tile.astype(F32) * SCALE
        high = tile.astype(BF16)
        low = (tile - high.astype(F32)).astype(BF16)
        return jnp.concatenate([high, low], axis=1)

    def step(score, weigh):
        if score is not None:
            c, b, h = score
            query = split(q[h, :, :, :, cut(c * HD, HD)].reshape(TOK, HD))
            peak = MX[h][c] if b else None
        if weigh is not None:
            cw, bw, hw = weigh
            top = M[hw][...]
            wide = jnp.tile(top, (1, SUB // HD))
            total = None
            if bw:
                fade = jnp.exp2(MX[hw][cw] - top)
                total = O[hw][cw] * jnp.concatenate([fade, fade], axis=1)
        for j in range(SLOTS // SUB):
            keys = slice(j * SUB, (j + 1) * SUB)
            if score is not None:
                block = lax.dot_general(
                    query, kd[b, keys, :], (((1,), (1,)), ((), ())), preferred_element_type=F32
                )
                S[h][:, keys] = block
                for t in range(SUB // HD):
                    part_of = block[:, t * HD : (t + 1) * HD]
                    peak = part_of if peak is None else jnp.maximum(peak, part_of)
            if weigh is not None:
                probs = jnp.exp2(S[hw][:, keys] - wide).astype(BF16)
                term = jnp.dot(probs, vd[bw, keys, :], preferred_element_type=F32)
                total = term if total is None else total + term
        if score is not None:
            M[h][...] = jnp.broadcast_to(jnp.max(peak, axis=1, keepdims=True), (TOK, HD))
        if weigh is not None:
            if bw:
                OF[hw][...] = total
                MF[hw][...] = top
            else:
                O[hw][cw] = total
                MX[hw][cw] = top

    def finish(h, c):
        weight = OF[h][:, HD:]
        part[h, c] = (OF[h][:, :HD] / weight).astype(BF16)
        lts[h, c] = (MF[h][...] + jnp.log(weight) * LOG2E).T[0:1, :]
        for d in (2, 1, 3):
            to, who = p_peer(h, d)
            remote(
                part.at[h, c, cut(to * 128, 128)], r1o.at[h, c, d - 1],
                rs_s.at[0, h, c], rs_r.at[0, h, c], who,
            ).start()
            remote(
                lts.at[h, c, :, cut(to * 128, 128)], r1l.at[h, c, d - 1],
                rl_s.at[0, h, c], rl_r.at[0, h, c], who,
            ).start()

    def spread(line):
        return jnp.broadcast_to(line, (HD, HD)).T

    def balance(logs):
        top = logs[0]
        for v in logs[1:]:
            top = jnp.maximum(top, v)
        weights = [jnp.exp2(v - top) for v in logs]
        total = weights[0]
        for v in weights[1:]:
            total = total + v
        return [v / total for v in weights], top + jnp.log(total) * LOG2E

    def join(parts, shares):
        summed = shares[0] * parts[0].astype(F32)
        for a, v in zip(parts[1:], shares[1:]):
            summed = summed + v * a.astype(F32)
        return summed.astype(BF16)

    def serve_1(h, c):
        await_bytes(r1o.at[h, c], rs_r.at[0, h, c])
        await_bytes(r1l.at[h, c], rl_r.at[0, h, c])
        p, s = place[h]
        shares, logs = balance(
            [lts[h, c, :, cut(p * 128, 128)]] + [r1l[h, c, i] for i in range(3)] + [fl[h, c]]
        )
        s2l[h, c] = logs
        s2o[h, c] = join(
            [part[h, c, cut(p * 128, 128), :]] + [r1o[h, c, i] for i in range(3)] + [fo[h, c]],
            [spread(v) for v in shares],
        )
        for d in (2, 1, 3):
            who = s_peer(h, d)[1]
            remote(
                s2o.at[h, c], r2o.at[h, c, d - 1], rs_s.at[1, h, c], rs_r.at[1, h, c], who
            ).start()
            remote(
                s2l.at[h, c], r2l.at[h, c, d - 1], rl_s.at[1, h, c], rl_r.at[1, h, c], who
            ).start()

    def serve_2(h, c):
        await_bytes(r2o.at[h, c], rs_r.at[1, h, c])
        await_bytes(r2l.at[h, c], rl_r.at[1, h, c])
        p, s = place[h]
        shares, _ = balance([s2l[h, c]] + [r2l[h, c, i] for i in range(3)])
        joined = join(
            [s2o[h, c]] + [r2o[h, c, i] for i in range(3)], [spread(v) for v in shares]
        )
        ref = g.at[h, p, :, :, cut(c * HD, HD)]
        g[h, p, :, :, cut(c * HD, HD)] = joined.reshape(4, 32, HD)
        for d in (2, 1, 3):
            remote(ref, ref, ag_s.at[h, c], ag_r.at[h, c], p_peer(h, d)[1]).start()

    def serve_3(h, c):
        await_bytes(g.at[h, pl.ds(0, 3), :, :, cut(c * HD, HD)], ag_r.at[h, c])

    def fresh():
        keys = q[0, :, :, :, 1024:].reshape(TOK, HD)
        keys = jnp.concatenate([keys, keys], axis=1)
        values = jnp.concatenate(
            [q[1, zz, xx, :, 1024:] for xx in range(NX) for zz in range(NZ)], axis=0
        )
        values = jnp.concatenate([values, jnp.ones((TOK, HD), BF16)], axis=1)
        rows = []
        for h in range(2):
            for c in range(HEADS):
                rows.append(q[h, place[h][0], place[h][1], :, c * HD : (c + 1) * HD])
        query = split(jnp.concatenate(rows, axis=0))
        row = lax.broadcasted_iota(jnp.int32, (TOK, TOK), 0)
        lane = lax.broadcasted_iota(jnp.int32, (TOK, TOK), 1)
        token = ((x * 2 + (row // ROWS) % 2) * NZ + z) * ROWS + row % ROWS
        key_at = ((lane // 128 * 2 + (lane // ROWS) % 2) * NZ + (lane // 32) % 4) * ROWS + lane % ROWS
        score = lax.dot_general(query, keys, (((1,), (1,)), ((), ())), preferred_element_type=F32)
        score = jnp.where(key_at <= token, score, NEG)
        top = jnp.broadcast_to(jnp.max(score, axis=1, keepdims=True), (TOK, HD))
        probs = jnp.exp2(score - jnp.tile(top, (1, TOK // HD))).astype(BF16)
        total = jnp.dot(probs, values, preferred_element_type=F32)
        weight = total[:, HD:]
        part_of = (total[:, :HD] / weight).astype(BF16).reshape(2, HEADS, 32, HD)
        logs = (top + jnp.log(weight) * LOG2E).reshape(2, HEADS, 32, HD)
        for h in range(2):
            mine_32 = cut(place[h][1] * 32, 32)
            tmp[...] = jnp.full((HD, HD), NEG, F32)
            for c in range(HEADS):
                fo[h, c, mine_32, :] = part_of[h, c]
                tmp[mine_32, :] = logs[h, c]
                fl[h, c] = tmp[...].T[0:1, :]

    def serve(c, half):
        for lag, act in ((LAGS[2], serve_3), (LAGS[1], serve_2), (LAGS[0], serve_1)):
            h = (half - lag) % 2
            j = c - (lag + h - half) // 2

            @pl.when(jnp.logical_and(j >= 0, j < HEADS))
            def _(act=act, j=j, h=h):
                act(h, j)

    for h in range(2):
        q_done(h, 0)
    step((0, 0, 0), None)

    def own(c, _):
        step((c, 0, 1), (c, 0, 0))

        @pl.when(c == 1)
        def _():
            q_lines(2, (qn_r, qf_r))
            q_second(PIECES)

        for h in range(2):
            q_done(h, c + 1)

        step((c + 1, 0, 0), (c, 0, 1))
        return 0

    LAST = HEADS - 1
    lax.fori_loop(0, LAST, own, 0)
    step((LAST, 0, 1), (LAST, 0, 0))
    for h in range(2):
        await_bytes(q.at[h, :, pl.ds(0, 3), :, pl.ds(1024, HD)], qa_r.at[h, PIECES])
    fresh()

    for copy in swap[:3]:
        copy.wait_recv()
    swap[3].start()
    settle(1)
    step((0, 1, 0), (LAST, 0, 1))
    step((0, 1, 1), (0, 1, 0))

    def other(c, _):
        finish(0, c)
        step((c + 1, 1, 0), (c, 1, 1))
        serve(c, 0)
        finish(1, c)
        step((c + 1, 1, 1), (c + 1, 1, 0))
        serve(c, 1)
        return 0

    lax.fori_loop(0, LAST, other, 0)
    finish(0, LAST)
    step(None, (LAST, 1, 1))
    finish(1, LAST)

    def drain(c, _):
        serve(c, 0)
        serve(c, 1)
        return 0

    BREAK = (2 * HEADS - 1 + LAGS[1]) // 2 + 1
    lax.fori_loop(LAST, BREAK, drain, 0)

    def heads_of(cc, first, count):
        blocks = []
        cols = pl.ds(first * HD, count * HD)
        for ll in range(2):
            t = ll * 2 + cc
            blocks.append(
                jnp.concatenate(
                    [
                        g[0, t, :, :, cols].reshape(128, count * HD),
                        g[1, :, t, :, cols].reshape(128, count * HD),
                    ],
                    axis=1,
                )
            )
        return jnp.concatenate(blocks, axis=0)

    def project(heads, k, first, count):
        size = count * HD
        top = jnp.dot(heads[:, :size], w[k, pl.ds(first * HD, size)], preferred_element_type=F32)
        return top + jnp.dot(
            heads[:, size:], w[k, pl.ds(1024 + first * HD, size)], preferred_element_type=F32
        )

    own_w.wait()
    for k in (yh, oh):
        if k is oh:
            swap[3].wait_recv()
        for a, cc in enumerate((1 - core, core)):
            acc[a, k] = project(heads_of(cc, 0, EARLY), k, 0, EARLY)

    lax.fori_loop(BREAK, (2 * HEADS - 1 + LAGS[2]) // 2 + 1, drain, 0)

    to_core = []
    late = HEADS - EARLY
    for k in (oh, yh):
        es1[k] = (acc[0, k] + project(heads_of(1 - core, EARLY, late), k, EARLY, late)).astype(BF16)
        copy = remote(es1.at[k], er1.at[k], c_s.at[k], c_r.at[k], sibling)
        copy.start()
        to_core.append(copy)
    last = []

    def send(i, ll, k):
        rows = cut(ll * 128, 128)
        es2[i] = (acc[1, k, rows, :] + er1[k, rows, :].astype(F32)).astype(BF16)
        copy = remote(es2.at[i], er2.at[i], e_s.at[i], e_r.at[i], ends[i])
        copy.start()
        last.append(copy)

    acc[1, oh] += project(heads_of(core, EARLY, late), oh, EARLY, late)
    to_core[0].wait_recv()
    send(0, yl, oh)
    send(1, 1 - yl, oh)
    acc[1, yh] += project(heads_of(core, EARLY, late), yh, EARLY, late)
    to_core[1].wait_recv()
    send(2, 1 - yl, yh)
    rows = cut(yl * 128, 128)
    result = acc[1, yh, rows, :] + er1[yh, rows, :].astype(F32)
    for i in (2, 1, 0):
        last[i].wait_recv()
        result = result + er2[i].astype(F32)
    result = result.astype(BF16)
    for hh in range(2):
        for zz in range(NZ):
            a, b = (zz * 2 + hh) * ROWS, (hh * NZ + zz) * ROWS
            out_ref[b : b + ROWS, :] = result[a : a + ROWS]

    for copy in to_core + last + swap:
        copy.wait_send()
    for i in range(3):
        q_lines(i, (qn_s, qf_s))
    for h in range(2):
        for i in range(PIECES + 1):
            start, size = SECOND[i]
            await_bytes(q.at[h, :, pl.ds(0, 3), :, pl.ds(start, size)], qa_s.at[h, i])

    def sent(c, _):
        cols = cut(c * HD, HD)
        for h in range(2):
            await_bytes(r1o.at[h, c], rs_s.at[0, h, c])
            await_bytes(r1l.at[h, c], rl_s.at[0, h, c])
            await_bytes(r2o.at[h, c], rs_s.at[1, h, c])
            await_bytes(r2l.at[h, c], rl_s.at[1, h, c])
            await_bytes(g.at[h, pl.ds(0, 3), :, :, cols], ag_s.at[h, c])
        return 0

    lax.fori_loop(0, HEADS, sent, 0)


def body(queries, new_keys, new_values, cache_keys, cache_values, cache_lens, out_weight):
    V = pltpu.VMEM
    D = pltpu.SemaphoreType.DMA
    any_ = pl.BlockSpec(memory_space=pl.ANY)
    return pl.pallas_call(
        kernel,
        out_shape=jax.ShapeDtypeStruct((128, 512), BF16),
        in_specs=[any_, any_, any_, any_, any_, pl.BlockSpec(memory_space=pltpu.SMEM), any_],
        out_specs=pl.BlockSpec(memory_space=pltpu.VMEM),
        scratch_shapes=[
            V((2, 4, 4, 32, 1152), BF16),
            V((2, SLOTS, 2 * HD), BF16),
            V((2, SLOTS, 2 * HD), BF16),
            V((2, 8, HD), jnp.int32),
            V((TOK, SLOTS), F32),
            V((TOK, SLOTS), F32),
            V((TOK, HD), F32),
            V((TOK, HD), F32),
            V((HEADS, TOK, 2 * HD), F32),
            V((HEADS, TOK, 2 * HD), F32),
            V((HEADS, TOK, HD), F32),
            V((HEADS, TOK, HD), F32),
            V((TOK, 2 * HD), F32),
            V((TOK, 2 * HD), F32),
            V((TOK, HD), F32),
            V((TOK, HD), F32),
            V((2, HEADS, HD, HD), BF16),
            V((2, HEADS, 1, HD), F32),
            V((2, HEADS, TOK, HD), BF16),
            V((2, HEADS, 1, TOK), F32),
            V((2, HEADS, 3, 128, HD), BF16),
            V((2, HEADS, 3, 1, 128), F32),
            V((2, HEADS, 128, HD), BF16),
            V((2, HEADS, 1, 128), F32),
            V((2, HEADS, 3, 128, HD), BF16),
            V((2, HEADS, 3, 1, 128), F32),
            V((HD, HD), F32),
            V((2, 4, 4, 32, 1024), BF16),
            V((2, 2048, 512), BF16),
            V((2, 2, 256, 512), F32),
            V((2, 256, 512), BF16),
            V((2, 256, 512), BF16),
            V((3, 128, 512), BF16),
            V((3, 128, 512), BF16),
            D((7,)),
            D((4,)),
            D((4,)),
            D((2, 3)),
            D((2, 3)),
            D((2, 3)),
            D((2, 3)),
            D((2, PIECES + 1)),
            D((2, PIECES + 1)),
            D((2, 2, HEADS)),
            D((2, 2, HEADS)),
            D((2, 2, HEADS)),
            D((2, 2, HEADS)),
            D((2, HEADS)),
            D((2, HEADS)),
            D((2,)),
            D((2,)),
            D((3,)),
            D((3,)),
        ],
        compiler_params=pltpu.CompilerParams(
            collective_id=0, has_side_effects=True, vmem_limit_bytes=60 << 20
        ),
        cost_estimate=pl.CostEstimate(flops=20 << 30, bytes_accessed=16 << 20, transcendentals=40 << 20),
    )(queries, new_keys, new_values, cache_keys, cache_values, cache_lens, out_weight)


def solution(mesh):
    in_specs = (
        P("ctx", "tp"),
        P("ctx", "tp"),
        P("ctx", "tp"),
        P("ctx", "tp"),
        P("ctx", "tp"),
        P("ctx"),
        P("tp", "ctx"),
    )
    return jax.shard_map(body, mesh=mesh, in_specs=in_specs, out_specs=P("tp", "ctx"), check_vma=False)
```
